32 devices in a mesh: groups: 2 (over x), rows: 16 (over z, y, core).
Axes of the slice: x: 2, y: 2, z: 4, core: 2. Of those that a mesh axis runs over, the one named last changes fastest.
Arguments:
- planes: bfloat16 [6, 48, 48, 256], P('groups', 'rows'), parts along dimension 0, may hold values from -6 to 6
- conv_weight: bfloat16 [3, 3, 3, 256, 256], P(None, None, None, 'rows'), may hold values from -0.125 to 0.125
Outputs:
- mixed: bfloat16 [6, 48, 48, 256], P('groups', 'rows'), parts along dimension 0
The draws below stay inside these ranges and needn't reach their ends.
There are 2 independent parts, one for each index of `groups`. The reference program is written for one: setup_inputs(seed, part) draws one part's arguments, and reference() takes and returns one part's arrays. A program takes and returns all parts, laid end to end along the dimension named above; an argument that names none is the same for every part. Nothing has to cross between parts.
All inputs are finite; a program needn't handle non-finite values.
Results may differ from the reference program's by a relative error of at most 0.0034.
Values may be sent and summed in bfloat16 or wider, within the bound.
A program may use at most 128 MiB of HBM per device.

```python
import jax
import jax.numpy as jnp
from jax import lax

C = 256
R = 48


def spiked(values, key, source, target, blocks, factor):
    owner, partner = [(jnp.arange(values.shape[dim]) // (values.shape[dim] // blocks)).reshape([-1 if axis == dim else 1 for axis in range(values.ndim)]) for dim in (source, target)]
    chosen = jax.random.permutation(key, blocks)[partner]
    strong = (owner == chosen) | (owner == (partner + blocks // 2) % blocks)
    return jnp.where(strong, factor * values, values)


def block_scale(own_key, extent, shards, low, top_value):
    def one(axis_at, shards_of):
        draws = jax.random.uniform(jax.random.fold_in(jax.random.fold_in(own_key, 6), axis_at), (shards_of,), jnp.float32, low / len(shards), top_value / len(shards))
        return jnp.repeat(jnp.exp(draws), extent[axis_at] // shards_of).reshape((-1,) + (1,) * (len(extent) - axis_at - 1))

    level = one(*shards[0])
    for cut in shards[1:]:
        level = level * one(*cut)
    return level


def scatter_about(rng, extent, deviation, limit, cuts=(), held_as=jnp.bfloat16):
    entries = jax.random.normal(rng, extent, jnp.float32) * deviation
    if len(cuts) > 0:
        entries = block_scale(rng, extent, cuts, -0.22, 0.18) * entries
    return jnp.clip(entries, min=-limit, max=limit).astype(held_as)


def heavy_noise(rng, shape, width, limit, pieces, heavy, held_as=jnp.bfloat16):
    array = width * jax.random.normal(rng, shape, jnp.float32)
    if pieces:
        array = array * block_scale(rng, shape, pieces, -0.22, 0.18)
    return jnp.clip(spiked(array, jax.random.fold_in(rng, 3), *heavy), -limit, limit).astype(held_as)


def setup_inputs(seed: int = 0, part: int = 0) -> dict:
    streams_of = jax.random.split(jax.random.key(seed), 3)
    own_keys = jax.random.split(jax.random.fold_in(streams_of[2], part), 3)
    planes = heavy_noise(own_keys[0], (3, R, R, C), 1.0, 6.0, ((1, 16),), (1, 2, 16, 2.0))
    conv_weight = scatter_about(streams_of[1], (3, 3, 3, C, C), (9 * C) ** -0.5, 0.125, ((3, 16),))
    return {"planes": planes, "conv_weight": conv_weight}


def conv_plane(features, weight_all):
    out = lax.conv_general_dilated(features[None].astype(jnp.float32), weight_all.astype(jnp.float32), (1, 1), "SAME", dimension_numbers=("NHWC", "HWIO", "NHWC"), precision=lax.Precision.HIGHEST)
    return out[0].astype(jnp.bfloat16)


def reference(planes, conv_weight):
    plane_a, plane_b, plane_c = planes[0], planes[1], planes[2]

    def rowmean(plane):
        return (jnp.sum(plane, axis=1, dtype=jnp.float32) / R).astype(jnp.bfloat16)

    def colmean(plane):
        return (jnp.sum(plane, axis=0, dtype=jnp.float32) / R).astype(jnp.bfloat16)

    row_lines = [rowmean(plane_b), rowmean(plane_a), colmean(plane_a)]
    col_lines = [rowmean(plane_c), colmean(plane_c), colmean(plane_b)]
    weight_all = jnp.concatenate([conv_weight[0], conv_weight[1], conv_weight[2]], axis=2)
    results = []
    for index in range(3):
        plane = planes[index]
        upper = jnp.broadcast_to(row_lines[index][:, None, :], plane.shape)
        lower = jnp.broadcast_to(col_lines[index][None, :, :], plane.shape)
        features = jnp.concatenate([plane, upper, lower], axis=2)
        results.append(conv_plane(features, weight_all))
    return jnp.stack(results, axis=0)
```

```python
import functools

import jax
import jax.numpy as jnp
from jax import lax
from jax.experimental import pallas as pl
from jax.experimental.pallas import tpu as pltpu
from jax.sharding import PartitionSpec as P

MESH = pl.DeviceIdType.MESH
PAD = 16


def fused(n, split, planes, w, out, wbuf, xpad, cown, crecv, lsend, lines, vbuf, ubuf, ybuf,
          wsend, wrecv, hsend, hrecv, csem, crsem, lsem, lrsem):
    band, width, chans = planes.shape[1:]
    count = w.shape[1]
    nz = n // 4
    g = lax.axis_index("groups")
    me = lax.axis_index("rows")
    z, y, core = me // 4, (me // 2) % 2, me % 2

    def rank(zz, yy, cc):
        return (zz * 2 + yy) * 2 + cc

    partner = (g, rank(z, y, 1 - core))
    across = (g, rank(z, 1 - y, core))
    above = (g, lax.rem(me + 4, n))
    below = (g, lax.rem(me + n - 4, n))
    twin = (1 - g, me)

    barrier = pltpu.get_barrier_semaphore()
    for off in range(1, n):
        pl.semaphore_signal(barrier, inc=1, device_id=(g, lax.rem(me + off, n)), device_id_type=MESH)
    if split:
        pl.semaphore_signal(barrier, inc=1, device_id=twin, device_id_type=MESH)

    wbuf[:, pl.ds(pl.multiple_of(me * count, count), count), :] = w[...]
    xpad[:, 1:band + 1] = planes[...]

    @pl.when(me == 0)
    def _():
        xpad[:, 0] = jnp.zeros((3, width, chans), xpad.dtype)

    @pl.when(me == n - 1)
    def _():
        xpad[:, band + 1] = jnp.zeros((3, width, chans), xpad.dtype)

    pl.semaphore_wait(barrier, n if split else n - 1)

    sends = []

    def start(cond, k, s, dev):
        region = wbuf.at[pl.ds(9 * k, 9), pl.ds(pl.multiple_of(s * count, count), count), :]
        copy = pltpu.make_async_remote_copy(
            src_ref=region, dst_ref=region, send_sem=wsend.at[len(sends)], recv_sem=wrecv.at[k, s],
            device_id=dev, device_id_type=MESH)
        pl.when(cond)(copy.start)
        sends.append((cond, copy))

    def landed(k, s):
        region = wbuf.at[pl.ds(9 * k, 9), pl.ds(pl.multiple_of(s * count, count), count), :]
        pltpu.make_async_remote_copy(
            src_ref=region, dst_ref=region, send_sem=wsend.at[0], recv_sem=wrecv.at[k, s],
            device_id=partner, device_id_type=MESH).wait_recv()

    always = me >= 0

    def mine(zz):
        return lax.rem(zz + g, 2) == 0 if split else zz >= 0

    def along(k, zz, up, down, valid):
        s = rank(zz, y, core)
        if up:
            start(valid & (z < nz - 1), k, s, above)
        if down:
            start(valid & (z > 0), k, s, below)
        start(valid & mine(zz), k, s, across)
        start(valid, k, s, partner)

    def sideways(k, zz, valid):
        s = rank(zz, 1 - y, core)

        @pl.when(valid & mine(zz))
        def _():
            landed(k, s)
        if split:
            start(valid & mine(zz), k, s, twin)
        start(valid & mine(zz), k, s, partner)

    def third(k, zz, valid):
        s = rank(zz, 1 - y, core)
        cond = valid & jnp.logical_not(mine(zz))

        @pl.when(cond)
        def _():
            landed(k, s)
        start(cond, k, s, partner)

    for k in range(3):
        along(k, z, True, True, always)

    low = pltpu.make_async_remote_copy(
        src_ref=planes.at[:, band - 1], dst_ref=xpad.at[:, 0], send_sem=hsend.at[0], recv_sem=hrecv.at[0],
        device_id=(g, lax.rem(me + 1, n)), device_id_type=MESH)
    high = pltpu.make_async_remote_copy(
        src_ref=planes.at[:, 0], dst_ref=xpad.at[:, band + 1], send_sem=hsend.at[1], recv_sem=hrecv.at[1],
        device_id=(g, lax.rem(me + n - 1, n)), device_id_type=MESH)
    pl.when(me < n - 1)(low.start)
    pl.when(me > 0)(high.start)

    for p in range(3):
        total = planes[p, 0].astype(jnp.float32)
        for i in range(1, band):
            total = total + planes[p, i].astype(jnp.float32)
        for d in range(n):
            cown[d, p * band:(p + 1) * band, :] = total[d * band:(d + 1) * band, :]
    ccopies = []
    for off in range(1, n):
        peer = lax.rem(me + off, n)
        copy = pltpu.make_async_remote_copy(
            src_ref=cown.at[peer], dst_ref=crecv.at[off - 1], send_sem=csem.at[off - 1],
            recv_sem=crsem.at[off - 1], device_id=(g, peer), device_id_type=MESH)
        copy.start()
        ccopies.append(copy)
    lsend[...] = jnp.zeros(lsend.shape, lsend.dtype)
    rows = []
    for p in range(3):
        for i in range(band):
            rows.append(jnp.sum(planes[p, i].astype(jnp.float32), axis=0, keepdims=True) / width)
    for index, row in enumerate(rows):
        lsend[PAD + index:PAD + index + 1, :] = row

    def step(d):
        for k in range(3):
            for zz, up, down, valid in ((z - d, True, False, z - d >= 0), (z + d, False, True, z + d < nz)):
                s = rank(zz, y, core)

                @pl.when(valid)
                def _():
                    landed(k, s)
                along(k, zz, up, down, valid)
            for zz, valid in spread(d - 1):
                sideways(k, zz, valid)
            if split and d >= 2:
                for zz, valid in spread(d - 2):
                    third(k, zz, valid)

    def spread(d):
        if d == 0:
            return [(z, always)]
        return [(z - d, z - d >= 0), (z + d, z + d < nz)]

    step(1)

    for copy in ccopies:
        copy.wait_recv()
    total = cown[me][0:3 * band]
    for off in range(1, n):
        total = total + crecv[off - 1, 0:3 * band, :]
    lsend[0:3 * band, :] = total / width
    lines[me] = lsend[...].astype(jnp.bfloat16)
    lcopies = []
    for off in range(1, n):
        peer = lax.rem(me + off, n)
        copy = pltpu.make_async_remote_copy(
            src_ref=lines.at[me], dst_ref=lines.at[me], send_sem=lsem.at[off - 1],
            recv_sem=lrsem.at[me], device_id=(g, peer), device_id_type=MESH)
        copy.start()
        lcopies.append(copy)

    for d in range(2, nz):
        step(d)
    for k in range(3):
        for zz, valid in spread(nz - 1):
            sideways(k, zz, valid)
    if split:
        for d in (nz - 2, nz - 1):
            for k in range(3):
                for zz, valid in spread(d):
                    third(k, zz, valid)

    @pl.when(me > 0)
    def _():
        low.wait_recv()

    @pl.when(me < n - 1)
    def _():
        high.wait_recv()

    def gathered(k):
        for zz in range(nz):
            for yy in range(2):
                landed(k, rank(zz, yy, 1 - core))

    gathered(0)
    for b in range(3):
        for p in range(3):
            acc = None
            for a in range(3):
                lhs = xpad[p, a:a + band].reshape(band * width, chans)
                part = jnp.dot(lhs, wbuf[a * 3 + b], preferred_element_type=jnp.float32)
                acc = part if acc is None else acc + part
            ybuf[b, p] = acc.reshape(band, width, chans)

    for off in range(1, n):
        src = lax.rem(me + off, n)
        pltpu.make_async_remote_copy(
            src_ref=lines.at[src], dst_ref=lines.at[src], send_sem=lsem.at[0], recv_sem=lrsem.at[src],
            device_id=partner, device_id_type=MESH).wait_recv()
    vrows = (PAD + 2 * band, 2 * band, band)
    for s in range(n):
        block = lines[s].astype(jnp.float32)
        for p in range(3):
            vbuf[p * width + s * band:p * width + (s + 1) * band, :] = block[vrows[p]:vrows[p] + band, :]
    urows = (PAD + band, PAD, 0)
    before = lines[jnp.maximum(me - 1, 0)].astype(jnp.float32)
    here = lines[me].astype(jnp.float32)
    after = lines[jnp.minimum(me + 1, n - 1)].astype(jnp.float32)
    ubuf[...] = jnp.zeros(ubuf.shape, ubuf.dtype)
    depth = ubuf.shape[0] // 3
    for p in range(3):
        at = urows[p]
        ubuf[p * depth + 1:p * depth + 1 + band, :] = here[at:at + band, :]
        first = before[at + band - 1:at + band, :]
        last = after[at:at + 1, :]
        ubuf[p * depth:p * depth + 1, :] = jnp.where(me > 0, first, jnp.zeros_like(first))
        ubuf[p * depth + band + 1:p * depth + band + 2, :] = jnp.where(me < n - 1, last, jnp.zeros_like(last))

    gathered(1)
    gathered(2)
    ulhs = ubuf[...].astype(jnp.bfloat16)
    vlhs = vbuf[...].astype(jnp.bfloat16)
    u_all, v_all = [], []
    for b in range(3):
        u_all.append([jnp.dot(ulhs, wbuf[9 + a * 3 + b], preferred_element_type=jnp.float32) for a in range(3)])
    column = lax.broadcasted_iota(jnp.int32, (width, chans), 0)
    for p in range(3):
        vp = vlhs[p * width:(p + 1) * width]
        v_all = [[jnp.dot(vp, wbuf[18 + a * 3 + b], preferred_element_type=jnp.float32) for a in range(3)]
                 for b in range(3)]
        for i in range(band):
            terms = []
            for b in range(3):
                top, mid, bottom = v_all[b]
                if i == 0:
                    top = jnp.where(me > 0, top, jnp.zeros_like(top))
                if i == band - 1:
                    bottom = jnp.where(me < n - 1, bottom, jnp.zeros_like(bottom))
                line = sum(u_all[b][a][p * depth + i + a:p * depth + i + a + 1, :] for a in range(3))
                terms.append(ybuf[b, p, i] + (top + mid + bottom) + line)
            left = jnp.where(column == 0, 0.0, pltpu.roll(terms[0], 1, 0))
            right = jnp.where(column == width - 1, 0.0, pltpu.roll(terms[2], width - 1, 0))
            out[p, i] = (left + terms[1] + right).astype(out.dtype)

    for cond, copy in sends:
        pl.when(cond)(copy.wait_send)
    pl.when(me < n - 1)(low.wait_send)
    pl.when(me > 0)(high.wait_send)
    for copy in ccopies + lcopies:
        copy.wait_send()


def banded(n, split, planes, conv_weight):
    band, width, chans = planes.shape[1:]
    count = conv_weight.shape[3]
    depth = -(-(band + 2) // 8) * 8
    vmem = pl.BlockSpec(memory_space=pltpu.VMEM)
    dma = pltpu.SemaphoreType.DMA
    return pl.pallas_call(
        functools.partial(fused, n, split),
        out_shape=jax.ShapeDtypeStruct(planes.shape, planes.dtype),
        in_specs=[vmem, vmem],
        out_specs=vmem,
        scratch_shapes=[
            pltpu.VMEM((27, chans, chans), jnp.bfloat16),
            pltpu.VMEM((3, band + 2, width, chans), jnp.bfloat16),
            pltpu.VMEM((n, PAD, chans), jnp.float32),
            pltpu.VMEM((n - 1, PAD, chans), jnp.float32),
            pltpu.VMEM((2 * PAD, chans), jnp.float32),
            pltpu.VMEM((n, 2 * PAD, chans), jnp.bfloat16),
            pltpu.VMEM((3 * width, chans), jnp.float32),
            pltpu.VMEM((3 * depth, chans), jnp.float32),
            pltpu.VMEM((3, 3, band, width, chans), jnp.float32),
            dma((160,)), dma((3, n)), dma((2,)), dma((2,)),
            dma((n - 1,)), dma((n - 1,)), dma((n - 1,)), dma((n,)),
        ],
        compiler_params=pltpu.CompilerParams(
            collective_id=0, has_side_effects=True, vmem_limit_bytes=40 * 1024 * 1024),
    )(planes, conv_weight.reshape(27, count, chans))


def extended(block, sides, width):
    for axis, dim in sides:
        count = lax.axis_size(axis)
        forward = [(i, i + 1) for i in range(count - 1)]
        backward = [(target, source) for source, target in forward]
        low = lax.ppermute(
            lax.slice_in_dim(block, block.shape[dim] - width, None, axis=dim), axis, forward
        )
        high = lax.ppermute(lax.slice_in_dim(block, 0, width, axis=dim), axis, backward)
        block = jnp.concatenate([low, block, high], axis=dim)
    return block


def conv_block(padded, band, width, chans, piece):
    count = piece.shape[3]
    windows = []
    for block in range(3):
        sliced = lax.dynamic_slice_in_dim(padded, block * chans, count, 3)
        for krow in range(3):
            for kcol in range(3):
                windows.append(sliced[:, krow : krow + band, kcol : kcol + width, :])
    columns = jnp.concatenate(windows, axis=3)
    flat = piece.reshape(27 * count, chans)
    return jnp.einsum("prjc,cd->prjd", columns, flat, preferred_element_type=jnp.float32)


def body(planes, conv_weight):
    band = planes.shape[1]
    width = planes.shape[2]
    chans = planes.shape[3]
    row_sums = jnp.sum(planes, axis=2, dtype=jnp.float32)
    col_parts = jnp.sum(planes, axis=1, dtype=jnp.float32)
    line_u0 = (row_sums[1] / width).astype(jnp.bfloat16)
    line_u1 = (row_sums[0] / width).astype(jnp.bfloat16)
    means_yz = (row_sums[2] / width).astype(jnp.bfloat16)
    position = lax.axis_index("rows") * band
    totals = lax.psum((col_parts[0], col_parts[1], col_parts[2]), "rows")
    full_u2 = (totals[0] / width).astype(jnp.bfloat16)
    line_v1 = (totals[2] / width).astype(jnp.bfloat16)
    line_v2 = (totals[1] / width).astype(jnp.bfloat16)
    line_v0 = lax.all_gather(means_yz, "rows", axis=0, tiled=True)
    line_u2 = lax.dynamic_slice_in_dim(full_u2, position, band, 0)
    col_lines = jnp.stack([line_v0, line_v1, line_v2], axis=0)
    shape = planes.shape
    row_lines = jnp.stack([line_u0, line_u1, line_u2], axis=0)
    upper = jnp.broadcast_to(row_lines[:, :, None, :], shape)
    lower = jnp.broadcast_to(col_lines[:, None, :, :], shape)
    stacked = jnp.concatenate([planes, upper, lower], axis=3)
    padded = extended(stacked, (("rows", 1),), 1)
    padded = jnp.pad(padded, ((0, 0), (0, 0), (1, 1), (0, 0)))
    summed = conv_block(
        padded, band, width, chans, lax.all_gather(conv_weight, "rows", axis=3, tiled=True)
    )
    return summed.astype(jnp.bfloat16)


def solution(mesh):
    n = mesh.shape["rows"]
    split = mesh.shape["groups"] == 2

    def local(planes, conv_weight):
        band, width, chans = planes.shape[1:]
        fits = n % 4 == 0 and 3 * band <= PAD and width % 16 == 0 and conv_weight.shape[3] % 16 == 0
        if fits and band * n == width:
            return banded(n, split, planes, conv_weight)
        return body(planes, conv_weight)

    placed = (P("groups", "rows", None, None), P(None, None, None, "rows", None))
    return jax.shard_map(
        local, mesh=mesh, in_specs=placed, out_specs=P("groups", "rows", None, None), check_vma=False
    )
```

```python
import functools

import jax
import jax.numpy as jnp
from jax import lax
from jax.experimental import pallas as pl
from jax.experimental.pallas import tpu as pltpu
from jax.sharding import PartitionSpec as P

MESH = pl.DeviceIdType.MESH
PAD = 16


def fused(n, split, planes, w, out, wbuf, xpad, cown, cpart, crecv, lsend, lines, vbuf, ubuf, ybuf,
          wsend, wrecv, hsend, hrecv, psem, csem, crsem, lsem, lrsem, fsem, local):
    band, width, chans = planes.shape[1:]
    half = n // 2
    count = w.shape[1]
    nz = n // 4
    g = lax.axis_index("groups")
    me = lax.axis_index("rows")
    z, y, core = me // 4, (me // 2) % 2, me % 2

    def rank(zz, yy, cc):
        return (zz * 2 + yy) * 2 + cc

    partner = (g, rank(z, y, 1 - core))
    across = (g, rank(z, 1 - y, core))
    above = (g, lax.rem(me + 4, n))
    below = (g, lax.rem(me + n - 4, n))
    twin = (1 - g, me)

    own_planes = pltpu.make_async_copy(planes, xpad.at[:, pl.ds(1, band)], local.at[0])
    own_planes.start()
    own_weights = pltpu.make_async_copy(
        w, wbuf.at[:, pl.ds(pl.multiple_of(me * count, count), count), :], local.at[1])
    own_weights.start()

    def peer(off):
        return (g, lax.rem(me + 2 * off, n))

    barrier = pltpu.get_barrier_semaphore()
    greeted = [peer(off) for off in range(1, half)]
    greeted += [partner, (g, lax.rem(me + n - 1 + 2 * core, n))] + ([twin] if split else [])
    for device in greeted:
        pl.semaphore_signal(barrier, inc=1, device_id=device, device_id_type=MESH)

    @pl.when(me == 0)
    def _():
        xpad[:, 0] = jnp.zeros((3, width, chans), xpad.dtype)

    @pl.when(me == n - 1)
    def _():
        xpad[:, band + 1] = jnp.zeros((3, width, chans), xpad.dtype)

    own_planes.wait()
    for p in range(3):
        total = xpad[p, 1].astype(jnp.float32)
        for i in range(1, band):
            total = total + xpad[p, 1 + i].astype(jnp.float32)
        for d in range(n):
            cown[d % 2, d // 2, p * band:(p + 1) * band, :] = total[d * band:(d + 1) * band, :]
    pl.semaphore_wait(barrier, len(greeted))

    swap = pltpu.make_async_remote_copy(
        src_ref=cown.at[1 - core], dst_ref=cpart, send_sem=psem.at[0], recv_sem=psem.at[1],
        device_id=partner, device_id_type=MESH)
    swap.start()
    own_weights.wait()

    sends = []

    def start(cond, k, s, dev):
        region = wbuf.at[pl.ds(9 * k, 9), pl.ds(pl.multiple_of(s * count, count), count), :]
        copy = pltpu.make_async_remote_copy(
            src_ref=region, dst_ref=region, send_sem=wsend.at[len(sends)], recv_sem=wrecv.at[k, s],
            device_id=dev, device_id_type=MESH)
        pl.when(cond)(copy.start)
        sends.append((cond, copy))

    def landed(k, s):
        region = wbuf.at[pl.ds(9 * k, 9), pl.ds(pl.multiple_of(s * count, count), count), :]
        pltpu.make_async_remote_copy(
            src_ref=region, dst_ref=region, send_sem=wsend.at[0], recv_sem=wrecv.at[k, s],
            device_id=partner, device_id_type=MESH).wait_recv()

    always = me >= 0

    def mine(zz):
        return lax.rem(zz + g, 2) == 0 if split else zz >= 0

    def along(k, zz, up, down, valid, last=False):
        s = rank(zz, y, core)
        first = lax.rem(core + g, 2) == 0 if split else always
        if up:
            start(valid & (z < nz - 1) & (first if last else always), k, s, above)
        if down:
            start(valid & (z > 0) & (first if last else always), k, s, below)
        start(valid & mine(zz), k, s, across)
        start(valid, k, s, partner)

    def sideways(k, zz, valid):
        s = rank(zz, 1 - y, core)

        @pl.when(valid & mine(zz))
        def _():
            landed(k, s)
        if split:
            start(valid & mine(zz), k, s, twin)
        start(valid & mine(zz), k, s, partner)

    def third(k, zz, valid):
        s = rank(zz, 1 - y, core)
        cond = valid & jnp.logical_not(mine(zz))

        @pl.when(cond)
        def _():
            landed(k, s)
        start(cond, k, s, partner)

    along(0, z, True, True, always)
    swap.wait_recv()
    ccopies = []
    for q in range(half):
        cpart[q, 0:3 * band, :] = cpart[q, 0:3 * band, :] + cown[core, q, 0:3 * band, :]
    for off in range(1, half):
        copy = pltpu.make_async_remote_copy(
            src_ref=cpart.at[lax.rem(me // 2 + off, half)], dst_ref=crecv.at[off - 1],
            send_sem=csem.at[off - 1], recv_sem=crsem.at[off - 1],
            device_id=peer(off), device_id_type=MESH)
        copy.start()
        ccopies.append(copy)
    along(1, z, True, True, always)
    along(2, z, True, True, always)

    low = pltpu.make_async_remote_copy(
        src_ref=xpad.at[:, band], dst_ref=xpad.at[:, 0], send_sem=hsend.at[0], recv_sem=hrecv.at[0],
        device_id=(g, lax.rem(me + 1, n)), device_id_type=MESH)
    high = pltpu.make_async_remote_copy(
        src_ref=xpad.at[:, 1], dst_ref=xpad.at[:, band + 1], send_sem=hsend.at[1], recv_sem=hrecv.at[1],
        device_id=(g, lax.rem(me + n - 1, n)), device_id_type=MESH)
    pl.when(me < n - 1)(low.start)
    pl.when(me > 0)(high.start)

    lsend[...] = jnp.zeros(lsend.shape, lsend.dtype)
    for p in range(3):
        for i in range(band):
            row = jnp.sum(xpad[p, 1 + i].astype(jnp.float32), axis=0, keepdims=True) / width
            lsend[PAD + p * band + i:PAD + p * band + i + 1, :] = row

    def step(d):
        for k in range(3):
            for zz, up, down, valid in ((z - d, True, False, z - d >= 0), (z + d, False, True, z + d < nz)):
                s = rank(zz, y, core)

                @pl.when(valid)
                def _():
                    landed(k, s)
                if split and d == nz - 1:
                    start(valid & (lax.rem(core + g, 2) == 0), k, s, twin)
                along(k, zz, up, down, valid, d == nz - 2)
            for zz, valid in spread(d - 1):
                sideways(k, zz, valid)
            if split and d >= 2:
                for zz, valid in spread(d - 2):
                    third(k, zz, valid)

    def spread(d):
        if d == 0:
            return [(z, always)]
        return [(z - d, z - d >= 0), (z + d, z + d < nz)]

    for copy in ccopies:
        copy.wait_recv()
    total = cpart[me // 2, 0:3 * band, :]
    for off in range(1, half):
        total = total + crecv[off - 1, 0:3 * band, :]
    lsend[0:3 * band, :] = total / width
    lines[me] = lsend[...].astype(jnp.bfloat16)
    lcopies = []

    def send_line(src, sem, device):
        copy = pltpu.make_async_remote_copy(
            src_ref=lines.at[src], dst_ref=lines.at[src], send_sem=sem, recv_sem=lrsem.at[src],
            device_id=device, device_id_type=MESH)
        copy.start()
        lcopies.append(copy)

    def line_landed(src):
        pltpu.make_async_remote_copy(
            src_ref=lines.at[src], dst_ref=lines.at[src], send_sem=lsem.at[0], recv_sem=lrsem.at[src],
            device_id=partner, device_id_type=MESH).wait_recv()

    for off in range(1, half):
        send_line(me, lsem.at[off], peer(off))
    send_line(me, lsem.at[0], partner)

    step(1)
    if nz > 2:
        step(2)
    for off in range(1, half):
        src = lax.rem(me + 2 * off, n)
        line_landed(src)
        send_line(src, fsem.at[off - 1], partner)
    for d in range(3, nz):
        step(d)
    for k in range(3):
        for zz, valid in spread(nz - 1):
            sideways(k, zz, valid)
    if split:
        for d in (nz - 2, nz - 1):
            for k in range(3):
                for zz, valid in spread(d):
                    third(k, zz, valid)

    @pl.when(me > 0)
    def _():
        low.wait_recv()

    @pl.when(me < n - 1)
    def _():
        high.wait_recv()

    def gathered(k):
        for zz in range(nz):
            for yy in range(2):
                landed(k, rank(zz, yy, 1 - core))

    gathered(0)
    for b in range(3):
        for p in range(3):
            acc = None
            for a in range(3):
                lhs = xpad[p, a:a + band].reshape(band * width, chans)
                part = jnp.dot(lhs, wbuf[a * 3 + b], preferred_element_type=jnp.float32)
                acc = part if acc is None else acc + part
            ybuf[b, p] = acc.reshape(band, width, chans)

    for q in range(half):
        line_landed(2 * q + 1 - core)
    vrows = (PAD + 2 * band, 2 * band, band)
    for s in range(n):
        block = lines[s].astype(jnp.float32)
        for p in range(3):
            vbuf[p * width + s * band:p * width + (s + 1) * band, :] = block[vrows[p]:vrows[p] + band, :]
    urows = (PAD + band, PAD, 0)
    before = lines[jnp.maximum(me - 1, 0)].astype(jnp.float32)
    here = lines[me].astype(jnp.float32)
    after = lines[jnp.minimum(me + 1, n - 1)].astype(jnp.float32)
    ubuf[...] = jnp.zeros(ubuf.shape, ubuf.dtype)
    depth = ubuf.shape[0] // 3
    for p in range(3):
        at = urows[p]
        ubuf[p * depth + 1:p * depth + 1 + band, :] = here[at:at + band, :]
        first = before[at + band - 1:at + band, :]
        last = after[at:at + 1, :]
        ubuf[p * depth:p * depth + 1, :] = jnp.where(me > 0, first, jnp.zeros_like(first))
        ubuf[p * depth + band + 1:p * depth + band + 2, :] = jnp.where(me < n - 1, last, jnp.zeros_like(last))

    gathered(1)
    gathered(2)
    ulhs = ubuf[...].astype(jnp.bfloat16)
    vlhs = vbuf[...].astype(jnp.bfloat16)
    u_all, v_all = [], []
    for b in range(3):
        u_all.append([jnp.dot(ulhs, wbuf[9 + a * 3 + b], preferred_element_type=jnp.float32) for a in range(3)])
    column = lax.broadcasted_iota(jnp.int32, (width, chans), 0)
    for p in range(3):
        vp = vlhs[p * width:(p + 1) * width]
        v_all = [[jnp.dot(vp, wbuf[18 + a * 3 + b], preferred_element_type=jnp.float32) for a in range(3)]
                 for b in range(3)]
        for i in range(band):
            terms = []
            for b in range(3):
                top, mid, bottom = v_all[b]
                if i == 0:
                    top = jnp.where(me > 0, top, jnp.zeros_like(top))
                if i == band - 1:
                    bottom = jnp.where(me < n - 1, bottom, jnp.zeros_like(bottom))
                line = sum(u_all[b][a][p * depth + i + a:p * depth + i + a + 1, :] for a in range(3))
                terms.append(ybuf[b, p, i] + (top + mid + bottom) + line)
            left = jnp.where(column == 0, 0.0, pltpu.roll(terms[0], 1, 0))
            right = jnp.where(column == width - 1, 0.0, pltpu.roll(terms[2], width - 1, 0))
            out[p, i] = (left + terms[1] + right).astype(out.dtype)

    for cond, copy in sends:
        pl.when(cond)(copy.wait_send)
    pl.when(me < n - 1)(low.wait_send)
    pl.when(me > 0)(high.wait_send)
    swap.wait_send()
    for copy in ccopies + lcopies:
        copy.wait_send()


def banded(n, split, planes, conv_weight):
    band, width, chans = planes.shape[1:]
    count = conv_weight.shape[3]
    depth = -(-(band + 2) // 8) * 8
    vmem = pl.BlockSpec(memory_space=pltpu.VMEM)
    dma = pltpu.SemaphoreType.DMA
    return pl.pallas_call(
        functools.partial(fused, n, split),
        out_shape=jax.ShapeDtypeStruct(planes.shape, planes.dtype),
        in_specs=[pl.BlockSpec(memory_space=pltpu.HBM)] * 2,
        out_specs=vmem,
        scratch_shapes=[
            pltpu.VMEM((27, chans, chans), jnp.bfloat16),
            pltpu.VMEM((3, band + 2, width, chans), jnp.bfloat16),
            pltpu.VMEM((2, n // 2, PAD, chans), jnp.float32),
            pltpu.VMEM((n // 2, PAD, chans), jnp.float32),
            pltpu.VMEM((n // 2 - 1, PAD, chans), jnp.float32),
            pltpu.VMEM((2 * PAD, chans), jnp.float32),
            pltpu.VMEM((n, 2 * PAD, chans), jnp.bfloat16),
            pltpu.VMEM((3 * width, chans), jnp.float32),
            pltpu.VMEM((3 * depth, chans), jnp.float32),
            pltpu.VMEM((3, 3, band, width, chans), jnp.float32),
            dma((192,)), dma((3, n)), dma((2,)), dma((2,)), dma((2,)),
            dma((n // 2 - 1,)), dma((n // 2 - 1,)), dma((n // 2,)), dma((n,)), dma((n // 2 - 1,)), dma((2,)),
        ],
        compiler_params=pltpu.CompilerParams(
            collective_id=0, has_side_effects=True, vmem_limit_bytes=60 * 1024 * 1024),
    )(planes, conv_weight.reshape(27, count, chans))


def extended(block, sides, width):
    for axis, dim in sides:
        count = lax.axis_size(axis)
        forward = [(i, i + 1) for i in range(count - 1)]
        backward = [(target, source) for source, target in forward]
        low = lax.ppermute(
            lax.slice_in_dim(block, block.shape[dim] - width, None, axis=dim), axis, forward
        )
        high = lax.ppermute(lax.slice_in_dim(block, 0, width, axis=dim), axis, backward)
        block = jnp.concatenate([low, block, high], axis=dim)
    return block


def conv_block(padded, band, width, chans, piece):
    count = piece.shape[3]
    windows = []
    for block in range(3):
        sliced = lax.dynamic_slice_in_dim(padded, block * chans, count, 3)
        for krow in range(3):
            for kcol in range(3):
                windows.append(sliced[:, krow : krow + band, kcol : kcol + width, :])
    columns = jnp.concatenate(windows, axis=3)
    flat = piece.reshape(27 * count, chans)
    return jnp.einsum("prjc,cd->prjd", columns, flat, preferred_element_type=jnp.float32)


def body(planes, conv_weight):
    band = planes.shape[1]
    width = planes.shape[2]
    chans = planes.shape[3]
    row_sums = jnp.sum(planes, axis=2, dtype=jnp.float32)
    col_parts = jnp.sum(planes, axis=1, dtype=jnp.float32)
    line_u0 = (row_sums[1] / width).astype(jnp.bfloat16)
    line_u1 = (row_sums[0] / width).astype(jnp.bfloat16)
    means_yz = (row_sums[2] / width).astype(jnp.bfloat16)
    position = lax.axis_index("rows") * band
    totals = lax.psum((col_parts[0], col_parts[1], col_parts[2]), "rows")
    full_u2 = (totals[0] / width).astype(jnp.bfloat16)
    line_v1 = (totals[2] / width).astype(jnp.bfloat16)
    line_v2 = (totals[1] / width).astype(jnp.bfloat16)
    line_v0 = lax.all_gather(means_yz, "rows", axis=0, tiled=True)
    line_u2 = lax.dynamic_slice_in_dim(full_u2, position, band, 0)
    col_lines = jnp.stack([line_v0, line_v1, line_v2], axis=0)
    shape = planes.shape
    row_lines = jnp.stack([line_u0, line_u1, line_u2], axis=0)
    upper = jnp.broadcast_to(row_lines[:, :, None, :], shape)
    lower = jnp.broadcast_to(col_lines[:, None, :, :], shape)
    stacked = jnp.concatenate([planes, upper, lower], axis=3)
    padded = extended(stacked, (("rows", 1),), 1)
    padded = jnp.pad(padded, ((0, 0), (0, 0), (1, 1), (0, 0)))
    summed = conv_block(
        padded, band, width, chans, lax.all_gather(conv_weight, "rows", axis=3, tiled=True)
    )
    return summed.astype(jnp.bfloat16)


def solution(mesh):
    n = mesh.shape["rows"]
    split = mesh.shape["groups"] == 2

    def local(planes, conv_weight):
        band, width, chans = planes.shape[1:]
        fits = n % 8 == 0 and n > 8 and 3 * band <= PAD and width % 16 == 0 and conv_weight.shape[3] % 16 == 0
        if fits and band * n == width:
            return banded(n, split, planes, conv_weight)
        return body(planes, conv_weight)

    placed = (P("groups", "rows", None, None), P(None, None, None, "rows", None))
    return jax.shard_map(
        local, mesh=mesh, in_specs=placed, out_specs=P("groups", "rows", None, None), check_vma=False
    )
```

```python
import functools

import jax
import jax.numpy as jnp
from jax import lax
from jax.experimental import pallas as pl
from jax.experimental.pallas import tpu as pltpu
from jax.sharding import PartitionSpec as P

MESH = pl.DeviceIdType.MESH
PAD = 16
PIECES = 3
TAPS = 27 // PIECES


def fused(n, split, planes, w, out, wbuf, xpad, cown, cpart, crecv, lsend, lines, vbuf, ubuf, ybuf,
          wsend, wrecv, hsend, hrecv, psem, csem, crsem, lsem, lrsem, fsem, local):
    band, width, chans = planes.shape[1:]
    half = n // 2
    count = w.shape[1]
    nz = n // 4
    g = lax.axis_index("groups")
    me = lax.axis_index("rows")
    z, y, core = me // 4, (me // 2) % 2, me % 2

    def rank(zz, yy, cc):
        return (zz * 2 + yy) * 2 + cc

    partner = (g, rank(z, y, 1 - core))
    across = (g, rank(z, 1 - y, core))
    above = (g, lax.rem(me + 4, n))
    below = (g, lax.rem(me + n - 4, n))
    twin = (1 - g, me)

    own_planes = pltpu.make_async_copy(planes, xpad.at[:, pl.ds(1, band)], local.at[0])
    own_planes.start()
    own_weights = pltpu.make_async_copy(
        w, wbuf.at[:, pl.ds(pl.multiple_of(me * count, count), count), :], local.at[1])
    own_weights.start()

    def peer(off):
        return (g, lax.rem(me + 2 * off, n))

    barrier = pltpu.get_barrier_semaphore()
    greeted = [peer(off) for off in range(1, half)]
    greeted += [partner, (g, lax.rem(me + n - 1 + 2 * core, n))] + ([twin] if split else [])
    for device in greeted:
        pl.semaphore_signal(barrier, inc=1, device_id=device, device_id_type=MESH)

    @pl.when(me == 0)
    def _():
        xpad[:, 0] = jnp.zeros((3, width, chans), xpad.dtype)

    @pl.when(me == n - 1)
    def _():
        xpad[:, band + 1] = jnp.zeros((3, width, chans), xpad.dtype)

    own_planes.wait()
    for p in range(3):
        total = xpad[p, 1].astype(jnp.float32)
        for i in range(1, band):
            total = total + xpad[p, 1 + i].astype(jnp.float32)
        for d in range(n):
            cown[d % 2, d // 2, p * band:(p + 1) * band, :] = total[d * band:(d + 1) * band, :]
    pl.semaphore_wait(barrier, len(greeted))

    swap = pltpu.make_async_remote_copy(
        src_ref=cown.at[1 - core], dst_ref=cpart, send_sem=psem.at[0], recv_sem=psem.at[1],
        device_id=partner, device_id_type=MESH)
    swap.start()
    own_weights.wait()

    sends = []

    def start(cond, k, s, dev):
        region = wbuf.at[pl.ds(TAPS * k, TAPS), pl.ds(pl.multiple_of(s * count, count), count), :]
        copy = pltpu.make_async_remote_copy(
            src_ref=region, dst_ref=region, send_sem=wsend.at[len(sends)], recv_sem=wrecv.at[k, s],
            device_id=dev, device_id_type=MESH)
        pl.when(cond)(copy.start)
        sends.append((cond, copy))

    def landed(k, s):
        region = wbuf.at[pl.ds(TAPS * k, TAPS), pl.ds(pl.multiple_of(s * count, count), count), :]
        pltpu.make_async_remote_copy(
            src_ref=region, dst_ref=region, send_sem=wsend.at[0], recv_sem=wrecv.at[k, s],
            device_id=partner, device_id_type=MESH).wait_recv()

    always = me >= 0

    def mine(zz):
        return lax.rem(zz + g, 2) == 0 if split else zz >= 0

    def along(k, zz, up, down, valid, last=False):
        s = rank(zz, y, core)
        first = lax.rem(core + g, 2) == 0 if split else always
        if up:
            start(valid & (z < nz - 1) & (first if last else always), k, s, above)
        if down:
            start(valid & (z > 0) & (first if last else always), k, s, below)
        start(valid & mine(zz), k, s, across)
        start(valid, k, s, partner)

    def sideways(k, zz, valid):
        s = rank(zz, 1 - y, core)

        @pl.when(valid & mine(zz))
        def _():
            landed(k, s)
        if split:
            start(valid & mine(zz), k, s, twin)
        start(valid & mine(zz), k, s, partner)

    def third(k, zz, valid):
        s = rank(zz, 1 - y, core)
        cond = valid & jnp.logical_not(mine(zz))

        @pl.when(cond)
        def _():
            landed(k, s)
        start(cond, k, s, partner)

    along(0, z, True, True, always)
    swap.wait_recv()
    ccopies = []
    for q in range(half):
        cpart[q, 0:3 * band, :] = cpart[q, 0:3 * band, :] + cown[core, q, 0:3 * band, :]
    for off in range(1, half):
        copy = pltpu.make_async_remote_copy(
            src_ref=cpart.at[lax.rem(me // 2 + off, half)], dst_ref=crecv.at[off - 1],
            send_sem=csem.at[off - 1], recv_sem=crsem.at[off - 1],
            device_id=peer(off), device_id_type=MESH)
        copy.start()
        ccopies.append(copy)
    for k in range(1, PIECES):
        along(k, z, True, True, always)

    low = pltpu.make_async_remote_copy(
        src_ref=xpad.at[:, band], dst_ref=xpad.at[:, 0], send_sem=hsend.at[0], recv_sem=hrecv.at[0],
        device_id=(g, lax.rem(me + 1, n)), device_id_type=MESH)
    high = pltpu.make_async_remote_copy(
        src_ref=xpad.at[:, 1], dst_ref=xpad.at[:, band + 1], send_sem=hsend.at[1], recv_sem=hrecv.at[1],
        device_id=(g, lax.rem(me + n - 1, n)), device_id_type=MESH)
    pl.when(me < n - 1)(low.start)
    pl.when(me > 0)(high.start)

    lsend[...] = jnp.zeros(lsend.shape, lsend.dtype)
    for p in range(3):
        for i in range(band):
            row = jnp.sum(xpad[p, 1 + i].astype(jnp.float32), axis=0, keepdims=True) / width
            lsend[PAD + p * band + i:PAD + p * band + i + 1, :] = row

    def step(d):
        for k in range(PIECES):
            for zz, up, down, valid in ((z - d, True, False, z - d >= 0), (z + d, False, True, z + d < nz)):
                s = rank(zz, y, core)

                @pl.when(valid)
                def _():
                    landed(k, s)
                if split and d == nz - 1:
                    start(valid & (lax.rem(core + g, 2) == 0), k, s, twin)
                along(k, zz, up, down, valid, d == nz - 2)
            for zz, valid in spread(d - 1):
                sideways(k, zz, valid)
            if split and d >= 2:
                for zz, valid in spread(d - 2):
                    third(k, zz, valid)

    def spread(d):
        if d == 0:
            return [(z, always)]
        return [(z - d, z - d >= 0), (z + d, z + d < nz)]

    for copy in ccopies:
        copy.wait_recv()
    total = cpart[me // 2, 0:3 * band, :]
    for off in range(1, half):
        total = total + crecv[off - 1, 0:3 * band, :]
    lsend[0:3 * band, :] = total / width
    lines[me] = lsend[...].astype(jnp.bfloat16)
    lcopies = []

    def send_line(src, sem, device):
        copy = pltpu.make_async_remote_copy(
            src_ref=lines.at[src], dst_ref=lines.at[src], send_sem=sem, recv_sem=lrsem.at[src],
            device_id=device, device_id_type=MESH)
        copy.start()
        lcopies.append(copy)

    def line_landed(src):
        pltpu.make_async_remote_copy(
            src_ref=lines.at[src], dst_ref=lines.at[src], send_sem=lsem.at[0], recv_sem=lrsem.at[src],
            device_id=partner, device_id_type=MESH).wait_recv()

    for off in range(1, half):
        send_line(me, lsem.at[off], peer(off))
    send_line(me, lsem.at[0], partner)

    step(1)
    if nz > 2:
        step(2)
    for off in range(1, half):
        src = lax.rem(me + 2 * off, n)
        line_landed(src)
        send_line(src, fsem.at[off - 1], partner)
    for d in range(3, nz):
        step(d)
    for k in range(PIECES):
        for zz, valid in spread(nz - 1):
            sideways(k, zz, valid)
    if split:
        for d in (nz - 2, nz - 1):
            for k in range(PIECES):
                for zz, valid in spread(d):
                    third(k, zz, valid)

    @pl.when(me > 0)
    def _():
        low.wait_recv()

    @pl.when(me < n - 1)
    def _():
        high.wait_recv()

    def gathered(block):
        for k in range(block * PIECES // 3, (block + 1) * PIECES // 3):
            collected(k)

    def collected(k):
        for zz in range(nz):
            for yy in range(2):
                landed(k, rank(zz, yy, 1 - core))

    gathered(0)
    for b in range(3):
        for p in range(3):
            acc = None
            for a in range(3):
                lhs = xpad[p, a:a + band].reshape(band * width, chans)
                part = jnp.dot(lhs, wbuf[a * 3 + b], preferred_element_type=jnp.float32)
                acc = part if acc is None else acc + part
            ybuf[b, p] = acc.reshape(band, width, chans)

    for q in range(half):
        line_landed(2 * q + 1 - core)
    vrows = (PAD + 2 * band, 2 * band, band)
    for s in range(n):
        block = lines[s].astype(jnp.float32)
        for p in range(3):
            vbuf[p * width + s * band:p * width + (s + 1) * band, :] = block[vrows[p]:vrows[p] + band, :]
    urows = (PAD + band, PAD, 0)
    before = lines[jnp.maximum(me - 1, 0)].astype(jnp.float32)
    here = lines[me].astype(jnp.float32)
    after = lines[jnp.minimum(me + 1, n - 1)].astype(jnp.float32)
    ubuf[...] = jnp.zeros(ubuf.shape, ubuf.dtype)
    depth = ubuf.shape[0] // 3
    for p in range(3):
        at = urows[p]
        ubuf[p * depth + 1:p * depth + 1 + band, :] = here[at:at + band, :]
        first = before[at + band - 1:at + band, :]
        last = after[at:at + 1, :]
        ubuf[p * depth:p * depth + 1, :] = jnp.where(me > 0, first, jnp.zeros_like(first))
        ubuf[p * depth + band + 1:p * depth + band + 2, :] = jnp.where(me < n - 1, last, jnp.zeros_like(last))

    gathered(1)
    gathered(2)
    ulhs = ubuf[...].astype(jnp.bfloat16)
    vlhs = vbuf[...].astype(jnp.bfloat16)
    u_all, v_all = [], []
    for b in range(3):
        u_all.append([jnp.dot(ulhs, wbuf[9 + a * 3 + b], preferred_element_type=jnp.float32) for a in range(3)])
    column = lax.broadcasted_iota(jnp.int32, (width, chans), 0)
    for p in range(3):
        vp = vlhs[p * width:(p + 1) * width]
        v_all = [[jnp.dot(vp, wbuf[18 + a * 3 + b], preferred_element_type=jnp.float32) for a in range(3)]
                 for b in range(3)]
        for i in range(band):
            terms = []
            for b in range(3):
                top, mid, bottom = v_all[b]
                if i == 0:
                    top = jnp.where(me > 0, top, jnp.zeros_like(top))
                if i == band - 1:
                    bottom = jnp.where(me < n - 1, bottom, jnp.zeros_like(bottom))
                line = sum(u_all[b][a][p * depth + i + a:p * depth + i + a + 1, :] for a in range(3))
                terms.append(ybuf[b, p, i] + (top + mid + bottom) + line)
            left = jnp.where(column == 0, 0.0, pltpu.roll(terms[0], 1, 0))
            right = jnp.where(column == width - 1, 0.0, pltpu.roll(terms[2], width - 1, 0))
            out[p, i] = (left + terms[1] + right).astype(out.dtype)

    for cond, copy in sends:
        pl.when(cond)(copy.wait_send)
    pl.when(me < n - 1)(low.wait_send)
    pl.when(me > 0)(high.wait_send)
    swap.wait_send()
    for copy in ccopies + lcopies:
        copy.wait_send()


def banded(n, split, planes, conv_weight):
    band, width, chans = planes.shape[1:]
    count = conv_weight.shape[3]
    depth = -(-(band + 2) // 8) * 8
    vmem = pl.BlockSpec(memory_space=pltpu.VMEM)
    dma = pltpu.SemaphoreType.DMA
    return pl.pallas_call(
        functools.partial(fused, n, split),
        out_shape=jax.ShapeDtypeStruct(planes.shape, planes.dtype),
        in_specs=[pl.BlockSpec(memory_space=pltpu.HBM)] * 2,
        out_specs=vmem,
        scratch_shapes=[
            pltpu.VMEM((27, chans, chans), jnp.bfloat16),
            pltpu.VMEM((3, band + 2, width, chans), jnp.bfloat16),
            pltpu.VMEM((2, n // 2, PAD, chans), jnp.float32),
            pltpu.VMEM((n // 2, PAD, chans), jnp.float32),
            pltpu.VMEM((n // 2 - 1, PAD, chans), jnp.float32),
            pltpu.VMEM((2 * PAD, chans), jnp.float32),
            pltpu.VMEM((n, 2 * PAD, chans), jnp.bfloat16),
            pltpu.VMEM((3 * width, chans), jnp.float32),
            pltpu.VMEM((3 * depth, chans), jnp.float32),
            pltpu.VMEM((3, 3, band, width, chans), jnp.float32),
            dma((64 * PIECES,)), dma((PIECES, n)), dma((2,)), dma((2,)), dma((2,)),
            dma((n // 2 - 1,)), dma((n // 2 - 1,)), dma((n // 2,)), dma((n,)), dma((n // 2 - 1,)), dma((2,)),
        ],
        compiler_params=pltpu.CompilerParams(
            collective_id=0, has_side_effects=True, vmem_limit_bytes=60 * 1024 * 1024),
    )(planes, conv_weight.reshape(27, count, chans))


def extended(block, sides, width):
    for axis, dim in sides:
        count = lax.axis_size(axis)
        forward = [(i, i + 1) for i in range(count - 1)]
        backward = [(target, source) for source, target in forward]
        low = lax.ppermute(
            lax.slice_in_dim(block, block.shape[dim] - width, None, axis=dim), axis, forward
        )
        high = lax.ppermute(lax.slice_in_dim(block, 0, width, axis=dim), axis, backward)
        block = jnp.concatenate([low, block, high], axis=dim)
    return block


def conv_block(padded, band, width, chans, piece):
    count = piece.shape[3]
    windows = []
    for block in range(3):
        sliced = lax.dynamic_slice_in_dim(padded, block * chans, count, 3)
        for krow in range(3):
            for kcol in range(3):
                windows.append(sliced[:, krow : krow + band, kcol : kcol + width, :])
    columns = jnp.concatenate(windows, axis=3)
    flat = piece.reshape(27 * count, chans)
    return jnp.einsum("prjc,cd->prjd", columns, flat, preferred_element_type=jnp.float32)


def body(planes, conv_weight):
    band = planes.shape[1]
    width = planes.shape[2]
    chans = planes.shape[3]
    row_sums = jnp.sum(planes, axis=2, dtype=jnp.float32)
    col_parts = jnp.sum(planes, axis=1, dtype=jnp.float32)
    line_u0 = (row_sums[1] / width).astype(jnp.bfloat16)
    line_u1 = (row_sums[0] / width).astype(jnp.bfloat16)
    means_yz = (row_sums[2] / width).astype(jnp.bfloat16)
    position = lax.axis_index("rows") * band
    totals = lax.psum((col_parts[0], col_parts[1], col_parts[2]), "rows")
    full_u2 = (totals[0] / width).astype(jnp.bfloat16)
    line_v1 = (totals[2] / width).astype(jnp.bfloat16)
    line_v2 = (totals[1] / width).astype(jnp.bfloat16)
    line_v0 = lax.all_gather(means_yz, "rows", axis=0, tiled=True)
    line_u2 = lax.dynamic_slice_in_dim(full_u2, position, band, 0)
    col_lines = jnp.stack([line_v0, line_v1, line_v2], axis=0)
    shape = planes.shape
    row_lines = jnp.stack([line_u0, line_u1, line_u2], axis=0)
    upper = jnp.broadcast_to(row_lines[:, :, None, :], shape)
    lower = jnp.broadcast_to(col_lines[:, None, :, :], shape)
    stacked = jnp.concatenate([planes, upper, lower], axis=3)
    padded = extended(stacked, (("rows", 1),), 1)
    padded = jnp.pad(padded, ((0, 0), (0, 0), (1, 1), (0, 0)))
    summed = conv_block(
        padded, band, width, chans, lax.all_gather(conv_weight, "rows", axis=3, tiled=True)
    )
    return summed.astype(jnp.bfloat16)


def solution(mesh):
    n = mesh.shape["rows"]
    split = False

    def local(planes, conv_weight):
        band, width, chans = planes.shape[1:]
        fits = n % 8 == 0 and n > 8 and 3 * band <= PAD and width % 16 == 0 and conv_weight.shape[3] % 16 == 0
        if fits and band * n == width:
            return banded(n, split, planes, conv_weight)
        return body(planes, conv_weight)

    placed = (P("groups", "rows", None, None), P(None, None, None, "rows", None))
    return jax.shard_map(
        local, mesh=mesh, in_specs=placed, out_specs=P("groups", "rows", None, None), check_vma=False
    )
```
